32 devices in a mesh: parts: 2 (over y), chan: 16 (over z, x, core).
Axes of the slice: x: 2, y: 2, z: 4, core: 2. Of those that a mesh axis runs over, the one named last changes fastest.
Arguments:
- samples: bfloat16 [4096, 16, 512], P(('parts', 'chan')), parts along dimension 0, may hold values from -160 to 160
- pair_blocks: int32 [32, 2], P('parts'), parts along dimension 0, may hold values from 0 to 15, as said below
Outputs:
- cross: bfloat16 [32, 128, 2, 128, 128], P(('parts', 'chan')), parts along dimension 0
The draws below stay inside these ranges and needn't reach their ends.
There are 2 independent parts, one for each index of `parts`. The reference program is written for one: setup_inputs(seed, part) draws one part's arguments, and reference() takes and returns one part's arrays. A program takes and returns all parts, laid end to end along the dimension named above; each array names one. Nothing has to cross between parts.
Inputs may be any that keep to these rules, and one draw needn't show every extreme that they name: `pair_blocks`: each row names two channel blocks, the first no greater than the second and at most 4 blocks before it; no two rows are equal.
All inputs are finite; a program needn't handle non-finite values.
Results may differ from the reference program's by a relative error of at most 0.0064.
Values may be sent and summed in bfloat16 or wider, within the bound.
A program may use at most 128 MiB of HBM per device.

```python
import math
import jax
import jax.numpy as jnp
from jax import lax

WINDOWS = 16
SAMPLES = 512
FREQS = 128
BLOCK = 128
REACH = 4
SMOOTH = 4
CHANNELS = 2048
PAIRS = 16


def draw_samples(key, part):
    key = jax.random.fold_in(key, 11)
    keys = jax.random.split(key, 4)
    position = jnp.arange(CHANNELS, dtype=jnp.float32) / max(CHANNELS - 1, 1)
    gain = (1.0 + 2.0 * position) * jax.random.uniform(keys[0], (CHANNELS,), jnp.float32, 0.7, 1.3)
    level = jnp.exp(jax.random.uniform(keys[1], (CHANNELS,), jnp.float32, 0.0, math.log(10.0)))
    common = 3.0 * jnp.clip(jax.random.normal(keys[2], (WINDOWS, SAMPLES), jnp.float32), -4.0, 4.0)
    noise = jnp.clip(jax.random.normal(keys[3], (CHANNELS, WINDOWS, SAMPLES), jnp.float32), -4.0, 4.0)
    values = level[:, None, None] * noise + gain[:, None, None] * common[None]
    return values.astype(jnp.bfloat16)


def draw_pair_blocks(key, part):
    key = jax.random.fold_in(key, 23)
    keys = jax.random.split(key, 2)
    blocks_all = CHANNELS // BLOCK
    count = blocks_all * (REACH + 1)
    index = jnp.arange(count, dtype=jnp.int32)
    first = index // (REACH + 1)
    offset = index % (REACH + 1)
    second = first + offset
    valid = second < blocks_all
    ranked = jax.random.permutation(keys[0], count).astype(jnp.int32)
    forced_low = (first == 0) & (offset == 0)
    forced_high = (first == blocks_all - 1) & (offset == 0)
    score = jnp.where(forced_low, 0, jnp.where(forced_high, 1, jnp.where(valid, 2 + ranked, 2 + count + ranked))).astype(jnp.int32)
    picked = jnp.argsort(score)[:PAIRS]
    shuffled = picked[jax.random.permutation(keys[1], PAIRS)]
    return jnp.stack([first[shuffled], second[shuffled]], axis=1).astype(jnp.int32)


def setup_inputs(seed: int = 0, part: int = 0) -> dict:
    arg_keys = jax.random.split(jax.random.key(seed), 3)
    part_keys = jax.random.split(jax.random.fold_in(arg_keys[2], part), 3)
    return {
        "samples": draw_samples(jax.random.fold_in(jax.random.fold_in(arg_keys[2], part), 71), part),
        "pair_blocks": draw_pair_blocks(jax.random.fold_in(jax.random.fold_in(arg_keys[2], part), 71), part),
    }


def fourier_table(bins, length):
    positions = jnp.arange(length, dtype=jnp.int32)
    numbers = jnp.arange(1, bins + 1, dtype=jnp.int32)
    turns = (numbers[:, None] * positions[None, :] % length).astype(jnp.float32)
    phase = 2.0 * math.pi * turns / length
    taper = 0.5 - 0.5 * jnp.cos(2.0 * math.pi * positions.astype(jnp.float32) / length)
    table = jnp.stack([taper[None, :] * jnp.cos(phase), -taper[None, :] * jnp.sin(phase)], axis=1)
    return table.astype(jnp.bfloat16)

def band_matrix(bins):
    index = jnp.arange(bins, dtype=jnp.int32)
    near = (jnp.abs(index[:, None] - index[None, :]) <= SMOOTH).astype(jnp.float32)
    return near / lax.optimization_barrier(jnp.sum(near, axis=1, keepdims=True))

def whiten(spectra, common, band):
    demeaned = spectra - common[..., None]
    amplitude = jnp.sqrt(demeaned[:, :, 0, :] ** 2 + demeaned[:, :, 1, :] ** 2)
    smoothed = jnp.einsum('fg,gwc->fwc', band, amplitude, precision=lax.Precision.HIGHEST)
    level = lax.optimization_barrier(jnp.mean(amplitude, axis=0))
    denominator = smoothed + 0.05 * level[None] + 1e-06
    return (demeaned / denominator[:, :, None, :]).astype(jnp.bfloat16)

def cross_spectrum(first, second, scale):
    width = first.shape[2] // 2
    product = lax.dot_general(first.astype(jnp.float32), second.astype(jnp.float32), (((1,), (1,)), ((0,), (0,))))
    real_part = product[:, :width, :width] + product[:, width:, width:]
    imag_part = product[:, width:, :width] - product[:, :width, width:]
    return (jnp.stack([real_part, imag_part], axis=1) * scale).astype(jnp.bfloat16)

def reference(samples, pair_blocks):
    table = fourier_table(FREQS, SAMPLES).astype(jnp.float32)
    band = band_matrix(FREQS)
    grouped = samples.reshape(CHANNELS // BLOCK, BLOCK, WINDOWS, SAMPLES)

    def block_spectra(group):
        return jnp.einsum('fkl,cwl->fwkc', table, group.astype(jnp.float32))

    def add_block(carry, group):
        return (carry + lax.optimization_barrier(jnp.sum(block_spectra(group), axis=3)), None)
    total, unused = lax.scan(add_block, jnp.zeros((FREQS, WINDOWS, 2), jnp.float32), grouped)
    common = total / CHANNELS

    def whiten_block(group):
        return whiten(block_spectra(group), common, band)
    whitened = lax.map(whiten_block, grouped)
    scale = 1.0 / math.sqrt(WINDOWS)

    def one_pair(pair):
        first = whitened[pair[0]].reshape(FREQS, WINDOWS, 2 * BLOCK)
        second = whitened[pair[1]].reshape(FREQS, WINDOWS, 2 * BLOCK)
        return cross_spectrum(first, second, scale)
    return lax.map(one_pair, pair_blocks.astype(jnp.int32))
```

```python
import functools
import math

import jax
import jax.numpy as jnp
from jax import lax
from jax.experimental import pallas as pl
from jax.experimental.pallas import tpu as pltpu
from jax.sharding import PartitionSpec as P

FREQS = 128
BLOCK = 128
SMOOTH = 4
CHUNKS = 2
MESH = pl.DeviceIdType.MESH


def fourier_table(bins, length):
    positions = jnp.arange(length, dtype=jnp.int32)
    numbers = jnp.arange(1, bins + 1, dtype=jnp.int32)
    turns = (numbers[:, None] * positions[None, :] % length).astype(jnp.float32)
    phase = 2.0 * math.pi * turns / length
    taper = 0.5 - 0.5 * jnp.cos(2.0 * math.pi * positions.astype(jnp.float32) / length)
    table = jnp.stack([taper[None, :] * jnp.cos(phase), -taper[None, :] * jnp.sin(phase)], axis=0)
    return table.astype(jnp.bfloat16).reshape(2 * bins, length)


def radices(n):
    out = []
    while n > 1:
        r = 4 if n % 4 == 0 else (2 if n % 2 == 0 else n)
        out.append(r)
        n //= r
    return out


def split3(x):
    hi = x.astype(jnp.bfloat16)
    rest = x - hi.astype(jnp.float32)
    mid = rest.astype(jnp.bfloat16)
    lo = (rest - mid.astype(jnp.float32)).astype(jnp.bfloat16)
    return hi, mid, lo


NT = (((1,), (1,)), ((), ()))


def exchange_kernel(n, steps, pairs_ref, x_ref, table_ref, owned_ref, spec, sums, gather, wide, send,
                    ssum, rsum, ssem, rsem, ssem2, rsem2, *bufs):
    recv, stage = bufs[:CHUNKS], bufs[CHUNKS:]
    windows, chans, length = x_ref.shape
    freqs = table_ref.shape[0] // 2
    per = windows // CHUNKS
    rows = 2 * per
    me = lax.axis_index("chan")

    barrier = pltpu.get_barrier_semaphore()

    def greet(k, c):
        pl.semaphore_signal(barrier, inc=1, device_id={"chan": lax.rem(me + k, n)}, device_id_type=MESH)
        return c

    lax.fori_loop(1, n, greet, 0)

    which = lax.broadcasted_iota(jnp.int32, (windows, windows * chans), 1) // chans
    mine = lax.broadcasted_iota(jnp.int32, (windows, windows * chans), 0)
    pick = (which == mine).astype(jnp.float32).astype(jnp.bfloat16)
    sums[0] = jnp.dot(
        pick, x_ref[...].reshape(windows * chans, length), preferred_element_type=jnp.float32
    )
    pl.semaphore_wait(barrier, n - 1)

    def sum_copy(phase, stride, radix, j):
        digit = lax.rem(me // stride, radix)
        other = me + (lax.rem(digit + j, radix) - digit) * stride
        return pltpu.make_async_remote_copy(
            src_ref=sums.at[phase], dst_ref=gather.at[phase, j - 1],
            send_sem=ssum.at[phase, j - 1], recv_sem=rsum.at[phase, j - 1],
            device_id={"chan": other}, device_id_type=MESH)

    pending = []
    stride = 1
    for phase, radix in enumerate(steps):
        copies = [sum_copy(phase, stride, radix, j) for j in range(1, radix)]
        for copy in copies:
            copy.start()
        if phase == 0:
            for w in range(windows):
                spec[w] = lax.dot_general(
                    table_ref[...], x_ref[w], NT, preferred_element_type=jnp.float32)
        total = sums[phase]
        for j, copy in enumerate(copies):
            copy.wait_recv()
            total = total + gather[phase, j]
        sums[phase + 1] = total
        pending += copies
        stride *= radix
    mean = sums[len(steps)] / (chans * n)
    common = sum(
        lax.dot_general(table_ref[...], part, NT, preferred_element_type=jnp.float32)
        for part in reversed(split3(mean)))

    fi = lax.broadcasted_iota(jnp.int32, (freqs, freqs), 0)
    gi = lax.broadcasted_iota(jnp.int32, (freqs, freqs), 1)
    near = (jnp.abs(fi - gi) <= SMOOTH).astype(jnp.float32)
    weight = 1.0 / jnp.sum(near, axis=1, keepdims=True)
    near = near.astype(jnp.bfloat16)

    for chunk in range(CHUNKS):
        for v in range(per):
            w = chunk * per + v
            part = spec[w] - common[:, w:w + 1]
            re, im = part[:freqs], part[freqs:]
            amplitude = jnp.sqrt(re * re + im * im)
            hi = amplitude.astype(jnp.bfloat16)
            lo = (amplitude - hi.astype(jnp.float32)).astype(jnp.bfloat16)
            smoothed = (jnp.dot(near, hi, preferred_element_type=jnp.float32)
                        + jnp.dot(near, lo, preferred_element_type=jnp.float32)) * weight
            level = jnp.sum(amplitude, axis=0, keepdims=True) * (1.0 / freqs)
            scale = 1.0 / (smoothed + (0.05 * level + 1e-06))
            wide[chunk, pl.ds(v, freqs, stride=rows), :] = re * scale
            wide[chunk, pl.ds(per + v, freqs, stride=rows), :] = im * scale
        send[chunk] = wide[chunk].astype(jnp.bfloat16).reshape(send.shape[1:])

        def give(k, c, chunk=chunk):
            to = lax.rem(me + k, n)
            pltpu.make_async_remote_copy(
                src_ref=send.at[chunk, to], dst_ref=recv[chunk].at[me],
                send_sem=ssem.at[chunk], recv_sem=rsem.at[chunk],
                device_id={"chan": to}, device_id_type=MESH).start()
            return c

        lax.fori_loop(1, n, give, 0)
        recv[chunk][me] = send[chunk, me]

    def all_of(ref, sem):
        piece = ref.at[pl.ds(0, n - 1)]
        return pltpu.make_async_copy(piece, piece, sem)

    for chunk in range(CHUNKS):
        all_of(recv[chunk], rsem.at[chunk]).wait()

        def route(k, c, chunk=chunk):
            to = lax.rem(me + k, n)
            stage[chunk][to, 0] = recv[chunk][pairs_ref[to, 0]]
            stage[chunk][to, 1] = recv[chunk][pairs_ref[to, 1]]
            pltpu.make_async_remote_copy(
                src_ref=stage[chunk].at[to], dst_ref=owned_ref.at[chunk, me],
                send_sem=ssem2.at[chunk], recv_sem=rsem2.at[chunk],
                device_id={"chan": to}, device_id_type=MESH).start()
            return c

        lax.fori_loop(1, n, route, 0)
        owned_ref[chunk, me, 0] = recv[chunk][pairs_ref[me, 0]]
        owned_ref[chunk, me, 1] = recv[chunk][pairs_ref[me, 1]]

    for copy in pending:
        copy.wait_send()
    for chunk in range(CHUNKS):
        all_of(recv[chunk], ssem.at[chunk]).wait()
        all_of(stage[chunk], ssem2.at[chunk]).wait()
        all_of(stage[chunk], rsem2.at[chunk]).wait()


def exchange(x, pair_blocks, table, n):
    windows, chans, length = x.shape
    freqs = table.shape[0] // 2
    bins = freqs // n
    rows = 2 * windows // CHUNKS
    steps = radices(n)
    most = max(steps) - 1
    piece = (bins, rows, chans)
    bf, f32 = jnp.bfloat16, jnp.float32
    vmem = pl.BlockSpec(memory_space=pltpu.VMEM)
    dma = pltpu.SemaphoreType.DMA
    return pl.pallas_call(
        functools.partial(exchange_kernel, n, steps),
        out_shape=jax.ShapeDtypeStruct((CHUNKS, n, 2) + piece, bf),
        in_specs=[pl.BlockSpec(memory_space=pltpu.SMEM), vmem, vmem],
        out_specs=vmem,
        scratch_shapes=[
            pltpu.VMEM((windows, 2 * freqs, chans), f32),
            pltpu.VMEM((len(steps) + 1, windows, length), f32),
            pltpu.VMEM((len(steps), most, windows, length), f32),
            pltpu.VMEM((CHUNKS, freqs * rows, chans), f32),
            pltpu.VMEM((CHUNKS, n) + piece, bf),
            dma((len(steps), most)), dma((len(steps), most)),
            dma((CHUNKS,)), dma((CHUNKS,)), dma((CHUNKS,)), dma((CHUNKS,)),
        ]
        + [pltpu.VMEM((n,) + piece, bf) for _ in range(CHUNKS)]
        + [pltpu.VMEM((n, 2) + piece, bf) for _ in range(CHUNKS)],
        compiler_params=pltpu.CompilerParams(
            collective_id=0, has_side_effects=True, vmem_limit_bytes=48 * 1024 * 1024),
    )(pair_blocks, x, table)


def cross_kernel(scale, owned_ref, out_ref):
    chunks, group, _, bins, rows, chans = owned_ref.shape
    half = rows // 2
    for s in range(group):
        for f in range(bins):
            first = [owned_ref[c, s, 0, f] for c in range(chunks)]
            turned = []
            for block in first:
                wide = block.astype(jnp.float32)
                turned.append(jnp.concatenate([wide[half:], -wide[:half]], axis=0).astype(jnp.bfloat16))
            left = jnp.concatenate(
                [jnp.concatenate(first, axis=0), jnp.concatenate(turned, axis=0)], axis=1)
            right = jnp.concatenate([owned_ref[c, s, 1, f] for c in range(chunks)], axis=0)
            product = lax.dot_general(
                left, right, (((0,), (0,)), ((), ())), preferred_element_type=jnp.float32) * scale
            out_ref[0, s * bins + f] = product.reshape(2, chans, chans).astype(jnp.bfloat16)


def cross_spectra(owned, freqs, scale):
    chunks, n, two, bins, rows, chans = owned.shape
    group = max(1, 8 // bins)
    return pl.pallas_call(
        functools.partial(cross_kernel, scale),
        grid=(n // group,),
        out_shape=jax.ShapeDtypeStruct((1, freqs, 2, chans, chans), jnp.bfloat16),
        in_specs=[pl.BlockSpec((chunks, group, two, bins, rows, chans), lambda i: (0, i, 0, 0, 0, 0))],
        out_specs=pl.BlockSpec((1, group * bins, 2, chans, chans), lambda i: (0, i, 0, 0, 0)),
        compiler_params=pltpu.CompilerParams(vmem_limit_bytes=32 * 1024 * 1024),
    )(owned)


def shards(samples, pair_blocks):
    windows, length = samples.shape[1:]
    n = lax.axis_size("chan")
    table = fourier_table(FREQS, length)
    owned = exchange(jnp.swapaxes(samples, 0, 1), pair_blocks, table, n)
    return cross_spectra(owned, FREQS, 1.0 / math.sqrt(windows))


def solution(mesh):
    placed = (P(("parts", "chan"), None, None), P("parts", None))
    return jax.shard_map(
        shards,
        mesh=mesh,
        in_specs=placed,
        out_specs=P(("parts", "chan"), None, None, None, None),
        check_vma=False,
    )
```

```python
import functools
import math

import jax
import jax.numpy as jnp
from jax import lax
from jax.experimental import pallas as pl
from jax.experimental.pallas import tpu as pltpu
from jax.sharding import PartitionSpec as P

FREQS = 128
BLOCK = 128
SMOOTH = 4
CHUNKS = 4
MESH = pl.DeviceIdType.MESH


def fourier_table(bins, length):
    positions = jnp.arange(length, dtype=jnp.int32)
    numbers = jnp.arange(1, bins + 1, dtype=jnp.int32)
    turns = (numbers[:, None] * positions[None, :] % length).astype(jnp.float32)
    phase = 2.0 * math.pi * turns / length
    taper = 0.5 - 0.5 * jnp.cos(2.0 * math.pi * positions.astype(jnp.float32) / length)
    table = jnp.stack([taper[None, :] * jnp.cos(phase), -taper[None, :] * jnp.sin(phase)], axis=0)
    return table.astype(jnp.bfloat16).reshape(2 * bins, length)


def radices(n):
    out = []
    while n > 1:
        r = 4 if n % 4 == 0 else (2 if n % 2 == 0 else n)
        out.append(r)
        n //= r
    return out


def split3(x):
    hi = x.astype(jnp.bfloat16)
    rest = x - hi.astype(jnp.float32)
    mid = rest.astype(jnp.bfloat16)
    lo = (rest - mid.astype(jnp.float32)).astype(jnp.bfloat16)
    return hi, mid, lo


NT = (((1,), (1,)), ((), ()))


def exchange_kernel(n, copies_held, chunks, steps, pairs_ref, x_ref, table_ref, owned_ref, spec, sums, gather, wide, send,
                    ssum, rsum, ssem, rsem, ssem2, rsem2, *bufs):
    recv, stage = bufs[:chunks], bufs[chunks:]
    holders = n // copies_held
    windows, chans, length = x_ref.shape
    freqs = table_ref.shape[0] // 2
    me = lax.axis_index("chan")
    place = lax.rem(me, holders)
    base = me - place

    barrier = pltpu.get_barrier_semaphore()

    def greet(k, c):
        pl.semaphore_signal(barrier, inc=1, device_id={"chan": lax.rem(me + k, n)}, device_id_type=MESH)
        return c

    lax.fori_loop(1, n, greet, 0)

    which = lax.broadcasted_iota(jnp.int32, (windows, windows * chans), 1) // chans
    mine = lax.broadcasted_iota(jnp.int32, (windows, windows * chans), 0)
    pick = (which == mine).astype(jnp.float32).astype(jnp.bfloat16)
    sums[0] = jnp.dot(
        pick, x_ref[...].reshape(windows * chans, length), preferred_element_type=jnp.float32
    )
    pl.semaphore_wait(barrier, n - 1)

    def sum_copy(phase, stride, radix, j):
        digit = lax.rem(me // stride, radix)
        other = me + (lax.rem(digit + j, radix) - digit) * stride
        return pltpu.make_async_remote_copy(
            src_ref=sums.at[phase], dst_ref=gather.at[phase, j - 1],
            send_sem=ssum.at[phase, j - 1], recv_sem=rsum.at[phase, j - 1],
            device_id={"chan": other}, device_id_type=MESH)

    pending = []
    stride = 1
    for phase, radix in enumerate(steps):
        copies = [sum_copy(phase, stride, radix, j) for j in range(1, radix)]
        for copy in copies:
            copy.start()
        if phase == 0:
            for w in range(windows):
                spec[w] = lax.dot_general(
                    table_ref[...], x_ref[w], NT, preferred_element_type=jnp.float32)
        total = sums[phase]
        for j, copy in enumerate(copies):
            copy.wait_recv()
            total = total + gather[phase, j]
        sums[phase + 1] = total
        pending += copies
        stride *= radix
    mean = sums[len(steps)] / (chans * n)
    common = sum(
        lax.dot_general(table_ref[...], part, NT, preferred_element_type=jnp.float32)
        for part in reversed(split3(mean)))

    fi = lax.broadcasted_iota(jnp.int32, (freqs, freqs), 0)
    gi = lax.broadcasted_iota(jnp.int32, (freqs, freqs), 1)
    near = (jnp.abs(fi - gi) <= SMOOTH).astype(jnp.float32)
    weight = 1.0 / jnp.sum(near, axis=1, keepdims=True)
    near = near.astype(jnp.bfloat16)

    for w in range(windows):
        part = spec[w] - common[:, w:w + 1]
        re, im = part[:freqs], part[freqs:]
        amplitude = jnp.sqrt(re * re + im * im)
        hi = amplitude.astype(jnp.bfloat16)
        lo = (amplitude - hi.astype(jnp.float32)).astype(jnp.bfloat16)
        smoothed = (jnp.dot(near, hi, preferred_element_type=jnp.float32)
                    + jnp.dot(near, lo, preferred_element_type=jnp.float32)) * weight
        level = jnp.sum(amplitude, axis=0, keepdims=True) * (1.0 / freqs)
        scale = 1.0 / (smoothed + (0.05 * level + 1e-06))
        wide[pl.ds(w, freqs, stride=2 * windows), :] = re * scale
        wide[pl.ds(windows + w, freqs, stride=2 * windows), :] = im * scale
    send[...] = wide[...].astype(jnp.bfloat16).reshape(send.shape)

    for chunk in range(chunks):

        def give(k, c, chunk=chunk):
            to = lax.rem(me + n // 2 + k, n)

            @pl.when(to != me)
            def _():
                pltpu.make_async_remote_copy(
                    src_ref=send.at[lax.rem(to, holders), chunk], dst_ref=recv[chunk].at[me],
                    send_sem=ssem.at[chunk], recv_sem=rsem.at[chunk],
                    device_id={"chan": to}, device_id_type=MESH).start()

            return c

        lax.fori_loop(0, n, give, 0)
        recv[chunk][me] = send[place, chunk]

    def all_of(ref, sem, count):
        piece = ref.at[pl.ds(0, count)]
        return pltpu.make_async_copy(piece, piece, sem)

    for chunk in range(chunks):
        all_of(recv[chunk], rsem.at[chunk], n - 1).wait()

        def route(k, c, chunk=chunk):
            spot = lax.rem(place + k, holders)
            to = base + spot
            stage[chunk][spot, 0] = recv[chunk][pairs_ref[to, 0]]
            stage[chunk][spot, 1] = recv[chunk][pairs_ref[to, 1]]
            pltpu.make_async_remote_copy(
                src_ref=stage[chunk].at[spot], dst_ref=owned_ref.at[chunk, place],
                send_sem=ssem2.at[chunk], recv_sem=rsem2.at[chunk],
                device_id={"chan": to}, device_id_type=MESH).start()
            return c

        lax.fori_loop(1, holders, route, 0)
        owned_ref[chunk, place, 0] = recv[chunk][pairs_ref[me, 0]]
        owned_ref[chunk, place, 1] = recv[chunk][pairs_ref[me, 1]]

    for copy in pending:
        copy.wait_send()
    for chunk in range(chunks):
        all_of(recv[chunk], ssem.at[chunk], n - 1).wait()
        all_of(stage[chunk], ssem2.at[chunk], holders - 1).wait()
        all_of(stage[chunk], rsem2.at[chunk], holders - 1).wait()


def exchange(x, pair_blocks, table, n):
    windows, chans, length = x.shape
    freqs = table.shape[0] // 2
    copies_held = 2 if n % 2 == 0 and n > 2 else 1
    holders = n // copies_held
    chunks = min(CHUNKS, freqs // holders)
    steps = radices(n)
    most = max(steps) - 1
    piece = (freqs // holders // chunks, 2 * windows, chans)
    bf, f32 = jnp.bfloat16, jnp.float32
    vmem = pl.BlockSpec(memory_space=pltpu.VMEM)
    dma = pltpu.SemaphoreType.DMA
    return pl.pallas_call(
        functools.partial(exchange_kernel, n, copies_held, chunks, steps),
        out_shape=jax.ShapeDtypeStruct((chunks, holders, 2) + piece, bf),
        in_specs=[pl.BlockSpec(memory_space=pltpu.SMEM), vmem, vmem],
        out_specs=vmem,
        scratch_shapes=[
            pltpu.VMEM((windows, 2 * freqs, chans), f32),
            pltpu.VMEM((len(steps) + 1, windows, length), f32),
            pltpu.VMEM((len(steps), most, windows, length), f32),
            pltpu.VMEM((freqs * 2 * windows, chans), f32),
            pltpu.VMEM((holders, chunks) + piece, bf),
            dma((len(steps), most)), dma((len(steps), most)),
            dma((chunks,)), dma((chunks,)), dma((chunks,)), dma((chunks,)),
        ]
        + [pltpu.VMEM((n,) + piece, bf) for _ in range(chunks)]
        + [pltpu.VMEM((holders, 2) + piece, bf) for _ in range(chunks)],
        compiler_params=pltpu.CompilerParams(
            collective_id=0, has_side_effects=True, vmem_limit_bytes=48 * 1024 * 1024),
    )(pair_blocks, x, table)


def cross_kernel(scale, owned_ref, out_ref):
    chunks, group, _, bins, rows, chans = owned_ref.shape
    half = rows // 2
    for s in range(group):
        for c in range(chunks):
            for f in range(bins):
                first, second = owned_ref[c, s, 0, f], owned_ref[c, s, 1, f]
                turned = jnp.concatenate([-second[half:], second[:half]], axis=0)
                product = lax.dot_general(
                    first, jnp.concatenate([second, turned], axis=1),
                    (((0,), (0,)), ((), ())), preferred_element_type=jnp.float32)
                product = (product * scale).astype(jnp.bfloat16)
                at = (s * chunks + c) * bins + f
                out_ref[0, at, 0] = product[:, :chans]
                out_ref[0, at, 1] = product[:, chans:]


def cross_spectra(owned, freqs, scale):
    chunks, n, two, bins, rows, chans = owned.shape
    group = max(1, 8 // (bins * chunks))
    return pl.pallas_call(
        functools.partial(cross_kernel, scale),
        grid=(n // group,),
        out_shape=jax.ShapeDtypeStruct((1, freqs, 2, chans, chans), jnp.bfloat16),
        in_specs=[pl.BlockSpec((chunks, group, two, bins, rows, chans), lambda i: (0, i, 0, 0, 0, 0))],
        out_specs=pl.BlockSpec((1, group * bins * chunks, 2, chans, chans), lambda i: (0, i, 0, 0, 0)),
        compiler_params=pltpu.CompilerParams(vmem_limit_bytes=32 * 1024 * 1024),
    )(owned)


def shards(samples, pair_blocks):
    windows, length = samples.shape[1:]
    n = lax.axis_size("chan")
    table = fourier_table(FREQS, length)
    owned = exchange(jnp.swapaxes(samples, 0, 1), pair_blocks, table, n)
    return cross_spectra(owned, FREQS, 1.0 / math.sqrt(windows))


def solution(mesh):
    placed = (P(("parts", "chan"), None, None), P("parts", None))
    return jax.shard_map(
        shards,
        mesh=mesh,
        in_specs=placed,
        out_specs=P(("parts", "chan"), None, None, None, None),
        check_vma=False,
    )
```

```python
import functools
import math

import jax
import jax.numpy as jnp
import ml_dtypes
import numpy as np
from jax import lax
from jax.experimental import pallas as pl
from jax.experimental.pallas import tpu as pltpu
from jax.sharding import PartitionSpec as P

FREQS = 128
BLOCK = 128
SMOOTH = 4
CHUNKS = 4
MESH = pl.DeviceIdType.MESH


def fourier_table(bins, length):
    positions = np.arange(length)
    turns = np.arange(1, bins + 1)[:, None] * positions[None, :] % length
    phase = 2.0 * np.pi * turns / length
    taper = 0.5 - 0.5 * np.cos(2.0 * np.pi * positions / length)
    table = np.concatenate([taper * np.cos(phase), -taper * np.sin(phase)], axis=0)
    return jnp.asarray(table.astype(np.float32).astype(ml_dtypes.bfloat16))


def radices(n):
    out = []
    while n > 1:
        r = 4 if n % 4 == 0 else (2 if n % 2 == 0 else n)
        out.append(r)
        n //= r
    return out


def split3(x):
    hi = x.astype(jnp.bfloat16)
    rest = x - hi.astype(jnp.float32)
    mid = rest.astype(jnp.bfloat16)
    lo = (rest - mid.astype(jnp.float32)).astype(jnp.bfloat16)
    return hi, mid, lo


NT = (((1,), (1,)), ((), ()))


def exchange_kernel(n, copies_held, chunks, steps, pairs_hbm, x_hbm, table_ref, owned_ref, pairs_ref, x_ref,
                    turned, spec, sums, gather, wide, send,
                    load, own, ssum, rsum, ssem, rsem, ssem2, rsem2, *bufs):
    recv, stage = bufs[:chunks], bufs[chunks:]
    holders = n // copies_held
    chans, windows, length = x_ref.shape
    freqs = table_ref.shape[0] // 2
    me = lax.axis_index("chan")
    place = lax.rem(me, holders)
    base = me - place

    fetch = pltpu.make_async_copy(x_hbm, x_ref, load.at[0])
    fetch.start()
    fetch_pairs = pltpu.make_async_copy(pairs_hbm, pairs_ref, load.at[1])
    fetch_pairs.start()
    barrier = pltpu.get_barrier_semaphore()

    def greet(k, c):
        pl.semaphore_signal(barrier, inc=1, device_id={"chan": lax.rem(me + k, n)}, device_id_type=MESH)
        return c

    lax.fori_loop(1, n, greet, 0)

    which = lax.broadcasted_iota(jnp.int32, (windows, windows * chans), 1) % windows
    mine = lax.broadcasted_iota(jnp.int32, (windows, windows * chans), 0)
    pick = (which == mine).astype(jnp.float32).astype(jnp.bfloat16)
    fetch.wait()
    sums[0] = jnp.dot(
        pick, x_ref[...].reshape(windows * chans, length), preferred_element_type=jnp.float32
    )
    pl.semaphore_wait(barrier, n - 1)

    def sum_copy(phase, stride, radix, j):
        digit = lax.rem(me // stride, radix)
        other = me + (lax.rem(digit + j, radix) - digit) * stride
        return pltpu.make_async_remote_copy(
            src_ref=sums.at[phase], dst_ref=gather.at[phase, j - 1],
            send_sem=ssum.at[phase, j - 1], recv_sem=rsum.at[phase, j - 1],
            device_id={"chan": other}, device_id_type=MESH)

    pending = []
    stride = 1
    for phase, radix in enumerate(steps):
        copies = [sum_copy(phase, stride, radix, j) for j in range(1, radix)]
        for copy in copies:
            copy.start()
        if phase == 0:
            turned[...] = jnp.swapaxes(x_ref[...], 0, 1)
            for w in range(0, windows, 2):
                both = lax.dot_general(
                    table_ref[...], turned[w:w + 2].reshape(2 * chans, length), NT,
                    preferred_element_type=jnp.float32)
                spec[w] = both[:, :chans]
                spec[w + 1] = both[:, chans:]
        total = sums[phase]
        for j, copy in enumerate(copies):
            copy.wait_recv()
            total = total + gather[phase, j]
        sums[phase + 1] = total
        pending += copies
        stride *= radix
    mean = sums[len(steps)] / (chans * n)
    common = sum(
        lax.dot_general(table_ref[...], part, NT, preferred_element_type=jnp.float32)
        for part in reversed(split3(mean)))

    fi = lax.broadcasted_iota(jnp.int32, (freqs, freqs), 0)
    gi = lax.broadcasted_iota(jnp.int32, (freqs, freqs), 1)
    near = (jnp.abs(fi - gi) <= SMOOTH).astype(jnp.float32)
    weight = 1.0 / jnp.sum(near, axis=1, keepdims=True)
    near = near.astype(jnp.bfloat16)

    for w in range(windows):
        part = spec[w] - common[:, w:w + 1]
        re, im = part[:freqs], part[freqs:]
        amplitude = jnp.sqrt(re * re + im * im)
        hi = amplitude.astype(jnp.bfloat16)
        lo = (amplitude - hi.astype(jnp.float32)).astype(jnp.bfloat16)
        smoothed = (jnp.dot(near, hi, preferred_element_type=jnp.float32)
                    + jnp.dot(near, lo, preferred_element_type=jnp.float32)) * weight
        level = jnp.sum(amplitude, axis=0, keepdims=True) * (1.0 / freqs)
        scale = 1.0 / (smoothed + (0.05 * level + 1e-06))
        wide[pl.ds(w, freqs, stride=2 * windows), :] = re * scale
        wide[pl.ds(windows + w, freqs, stride=2 * windows), :] = im * scale
    send[...] = wide[...].astype(jnp.bfloat16).reshape(send.shape)

    for chunk in range(chunks):

        def give(k, c, chunk=chunk):
            to = lax.rem(me + n // 2 + k, n)

            @pl.when(to != me)
            def _():
                pltpu.make_async_remote_copy(
                    src_ref=send.at[lax.rem(to, holders), chunk], dst_ref=recv[chunk].at[me],
                    send_sem=ssem.at[chunk], recv_sem=rsem.at[chunk],
                    device_id={"chan": to}, device_id_type=MESH).start()

            return c

        lax.fori_loop(0, n, give, 0)
        recv[chunk][me] = send[place, chunk]

    kept = []

    def all_of(ref, sem, count):
        piece = ref.at[pl.ds(0, count)]
        return pltpu.make_async_copy(piece, piece, sem)

    fetch_pairs.wait()
    for chunk in range(chunks):
        all_of(recv[chunk], rsem.at[chunk], n - 1).wait()

        def route(k, c, chunk=chunk):
            spot = lax.rem(place + k, holders)
            to = base + spot
            stage[chunk][spot, 0] = recv[chunk][pairs_ref[to, 0]]
            stage[chunk][spot, 1] = recv[chunk][pairs_ref[to, 1]]
            pltpu.make_async_remote_copy(
                src_ref=stage[chunk].at[spot], dst_ref=owned_ref.at[chunk, place],
                send_sem=ssem2.at[chunk], recv_sem=rsem2.at[chunk],
                device_id={"chan": to}, device_id_type=MESH).start()
            return c

        lax.fori_loop(1, holders, route, 0)
        stage[chunk][place, 0] = recv[chunk][pairs_ref[me, 0]]
        stage[chunk][place, 1] = recv[chunk][pairs_ref[me, 1]]
        keep = pltpu.make_async_copy(
            stage[chunk].at[place], owned_ref.at[chunk, place], own.at[chunk])
        keep.start()
        kept.append(keep)

    for copy in pending:
        copy.wait_send()
    for copy in kept:
        copy.wait()
    for chunk in range(chunks):
        all_of(recv[chunk], ssem.at[chunk], n - 1).wait()
        all_of(stage[chunk], ssem2.at[chunk], holders - 1).wait()
        all_of(stage[chunk], rsem2.at[chunk], holders - 1).wait()


def exchange(x, pair_blocks, table, n):
    chans, windows, length = x.shape
    freqs = table.shape[0] // 2
    copies_held = 2 if n % 2 == 0 and n > 2 else 1
    holders = n // copies_held
    chunks = min(CHUNKS, freqs // holders)
    steps = radices(n)
    most = max(steps) - 1
    piece = (freqs // holders // chunks, 2 * windows, chans)
    bf, f32 = jnp.bfloat16, jnp.float32
    vmem = pl.BlockSpec(memory_space=pltpu.VMEM)
    anywhere = pl.BlockSpec(memory_space=pl.ANY)
    dma = pltpu.SemaphoreType.DMA
    return pl.pallas_call(
        functools.partial(exchange_kernel, n, copies_held, chunks, steps),
        out_shape=jax.ShapeDtypeStruct((chunks, holders, 2) + piece, bf),
        in_specs=[anywhere, anywhere, vmem],
        out_specs=anywhere,
        scratch_shapes=[
            pltpu.SMEM(pair_blocks.shape, jnp.int32),
            pltpu.VMEM(x.shape, bf),
            pltpu.VMEM((windows, chans, length), bf),
            pltpu.VMEM((windows, 2 * freqs, chans), f32),
            pltpu.VMEM((len(steps) + 1, windows, length), f32),
            pltpu.VMEM((len(steps), most, windows, length), f32),
            pltpu.VMEM((freqs * 2 * windows, chans), f32),
            pltpu.VMEM((holders, chunks) + piece, bf),
            dma((2,)), dma((chunks,)),
            dma((len(steps), most)), dma((len(steps), most)),
            dma((chunks,)), dma((chunks,)), dma((chunks,)), dma((chunks,)),
        ]
        + [pltpu.VMEM((n,) + piece, bf) for _ in range(chunks)]
        + [pltpu.VMEM((holders, 2) + piece, bf) for _ in range(chunks)],
        compiler_params=pltpu.CompilerParams(
            collective_id=0, has_side_effects=True, vmem_limit_bytes=48 * 1024 * 1024),
    )(pair_blocks, x, table)


def cross_kernel(scale, owned_ref, out_ref):
    chunks, group, _, bins, rows, chans = owned_ref.shape
    half = rows // 2
    exact = math.frexp(scale)[0] == 0.5
    for s in range(group):
        for c in range(chunks):
            for f in range(bins):
                first, second = owned_ref[c, s, 0, f], owned_ref[c, s, 1, f]
                if exact:
                    first = first * jnp.bfloat16(scale)
                turned = jnp.concatenate([-second[half:], second[:half]], axis=0)
                product = lax.dot_general(
                    first, jnp.concatenate([second, turned], axis=1),
                    (((0,), (0,)), ((), ())), preferred_element_type=jnp.float32)
                product = (product if exact else product * scale).astype(jnp.bfloat16)
                at = (s * chunks + c) * bins + f
                out_ref[0, at, 0] = product[:, :chans]
                out_ref[0, at, 1] = product[:, chans:]


def cross_spectra(owned, freqs, scale):
    chunks, n, two, bins, rows, chans = owned.shape
    group = max(1, 8 // (bins * chunks))
    return pl.pallas_call(
        functools.partial(cross_kernel, scale),
        grid=(n // group,),
        out_shape=jax.ShapeDtypeStruct((1, freqs, 2, chans, chans), jnp.bfloat16),
        in_specs=[pl.BlockSpec((chunks, group, two, bins, rows, chans), lambda i: (0, i, 0, 0, 0, 0))],
        out_specs=pl.BlockSpec((1, group * bins * chunks, 2, chans, chans), lambda i: (0, i, 0, 0, 0)),
        compiler_params=pltpu.CompilerParams(vmem_limit_bytes=32 * 1024 * 1024),
    )(owned)


def shards(samples, pair_blocks):
    windows, length = samples.shape[1:]
    n = lax.axis_size("chan")
    table = fourier_table(FREQS, length)
    owned = exchange(samples, pair_blocks, table, n)
    return cross_spectra(owned, FREQS, 1.0 / math.sqrt(windows))


def solution(mesh):
    placed = (P(("parts", "chan"), None, None), P("parts", None))
    return jax.shard_map(
        shards,
        mesh=mesh,
        in_specs=placed,
        out_specs=P(("parts", "chan"), None, None, None, None),
        check_vma=False,
    )
```

```python
import functools
import math

import jax
import jax.numpy as jnp
import ml_dtypes
import numpy as np
from jax import lax
from jax.experimental import pallas as pl
from jax.experimental.pallas import tpu as pltpu
from jax.sharding import PartitionSpec as P

FREQS = 128
BLOCK = 128
SMOOTH = 4
CHUNKS = 4
MESH = pl.DeviceIdType.MESH


def fourier_table(bins, length):
    positions = np.arange(length)
    turns = np.arange(1, bins + 1)[:, None] * positions[None, :] % length
    phase = 2.0 * np.pi * turns / length
    taper = 0.5 - 0.5 * np.cos(2.0 * np.pi * positions / length)
    table = np.concatenate([taper * np.cos(phase), -taper * np.sin(phase)], axis=0)
    return jnp.asarray(table.astype(np.float32).astype(ml_dtypes.bfloat16))


def radices(n):
    out = []
    while n > 1:
        r = 4 if n % 4 == 0 else (2 if n % 2 == 0 else n)
        out.append(r)
        n //= r
    return out


def split3(x):
    hi = x.astype(jnp.bfloat16)
    rest = x - hi.astype(jnp.float32)
    mid = rest.astype(jnp.bfloat16)
    lo = (rest - mid.astype(jnp.float32)).astype(jnp.bfloat16)
    return hi, mid, lo


NT = (((1,), (1,)), ((), ()))


def exchange_kernel(n, copies_held, chunks, steps, pairs_hbm, x_hbm, table_hbm, owned_ref, pairs_ref, x_ref,
                    table_ref, turned, spec, sums, gather, wide, send,
                    load, own, ssum, rsum, ssem, rsem, ssem2, rsem2, *bufs):
    recv, stage = bufs[:chunks], bufs[chunks:]
    holders = n // copies_held
    chans, windows, length = x_ref.shape
    freqs = table_ref.shape[0] // 2
    me = lax.axis_index("chan")
    place = lax.rem(me, holders)
    base = me - place

    fetch = pltpu.make_async_copy(x_hbm, x_ref, load.at[0])
    fetch.start()
    fetch_pairs = pltpu.make_async_copy(pairs_hbm, pairs_ref, load.at[1])
    fetch_pairs.start()
    fetch_table = pltpu.make_async_copy(table_hbm, table_ref, load.at[2])
    fetch_table.start()
    barrier = pltpu.get_barrier_semaphore()

    def greet(k, c):
        pl.semaphore_signal(barrier, inc=1, device_id={"chan": lax.rem(me + k, n)}, device_id_type=MESH)
        return c

    lax.fori_loop(1, n, greet, 0)

    which = lax.broadcasted_iota(jnp.int32, (windows, windows * chans), 1) % windows
    mine = lax.broadcasted_iota(jnp.int32, (windows, windows * chans), 0)
    pick = (which == mine).astype(jnp.float32).astype(jnp.bfloat16)
    fetch.wait()
    local = jnp.dot(
        pick, x_ref[...].reshape(windows * chans, length), preferred_element_type=jnp.float32
    )
    fetch_table.wait()
    sums[0] = sum(
        lax.dot_general(part, table_ref[...], NT, preferred_element_type=jnp.float32)
        for part in reversed(split3(local)))
    pl.semaphore_wait(barrier, n - 1)

    def sum_copy(phase, stride, radix, j):
        digit = lax.rem(me // stride, radix)
        other = me + (lax.rem(digit + j, radix) - digit) * stride
        return pltpu.make_async_remote_copy(
            src_ref=sums.at[phase], dst_ref=gather.at[phase, j - 1],
            send_sem=ssum.at[phase, j - 1], recv_sem=rsum.at[phase, j - 1],
            device_id={"chan": other}, device_id_type=MESH)

    pending = []
    stride = 1
    for phase, radix in enumerate(steps):
        copies = [sum_copy(phase, stride, radix, j) for j in range(1, radix)]
        for copy in copies:
            copy.start()
        if phase == 0:
            turned[...] = jnp.swapaxes(x_ref[...], 0, 1)
            for w in range(0, windows, 2):
                both = lax.dot_general(
                    table_ref[...], turned[w:w + 2].reshape(2 * chans, length), NT,
                    preferred_element_type=jnp.float32)
                spec[w] = both[:, :chans]
                spec[w + 1] = both[:, chans:]
        total = sums[phase]
        for j, copy in enumerate(copies):
            copy.wait_recv()
            total = total + gather[phase, j]
        sums[phase + 1] = total
        pending += copies
        stride *= radix
    common = (sums[len(steps)] / (chans * n)).T

    fi = lax.broadcasted_iota(jnp.int32, (freqs, freqs), 0)
    gi = lax.broadcasted_iota(jnp.int32, (freqs, freqs), 1)
    near = (jnp.abs(fi - gi) <= SMOOTH).astype(jnp.float32)
    weight = 1.0 / jnp.sum(near, axis=1, keepdims=True)
    near = near.astype(jnp.bfloat16)

    for w in range(windows):
        part = spec[w] - common[:, w:w + 1]
        re, im = part[:freqs], part[freqs:]
        amplitude = jnp.sqrt(re * re + im * im)
        hi = amplitude.astype(jnp.bfloat16)
        lo = (amplitude - hi.astype(jnp.float32)).astype(jnp.bfloat16)
        smoothed = (jnp.dot(near, hi, preferred_element_type=jnp.float32)
                    + jnp.dot(near, lo, preferred_element_type=jnp.float32)) * weight
        level = jnp.sum(amplitude, axis=0, keepdims=True) * (1.0 / freqs)
        scale = 1.0 / (smoothed + (0.05 * level + 1e-06))
        wide[pl.ds(w, freqs, stride=2 * windows), :] = re * scale
        wide[pl.ds(windows + w, freqs, stride=2 * windows), :] = im * scale
    send[...] = wide[...].astype(jnp.bfloat16).reshape(send.shape)

    for chunk in range(chunks):

        def give(k, c, chunk=chunk):
            to = lax.rem(me + n // 2 + k, n)

            @pl.when(to != me)
            def _():
                pltpu.make_async_remote_copy(
                    src_ref=send.at[lax.rem(to, holders), chunk], dst_ref=recv[chunk].at[me],
                    send_sem=ssem.at[chunk], recv_sem=rsem.at[chunk],
                    device_id={"chan": to}, device_id_type=MESH).start()

            return c

        lax.fori_loop(0, n, give, 0)
        recv[chunk][me] = send[place, chunk]

    kept = []

    def all_of(ref, sem, count):
        piece = ref.at[pl.ds(0, count)]
        return pltpu.make_async_copy(piece, piece, sem)

    fetch_pairs.wait()
    for chunk in range(chunks):
        all_of(recv[chunk], rsem.at[chunk], n - 1).wait()

        def route(k, c, chunk=chunk):
            spot = lax.rem(place + k, holders)
            to = base + spot
            stage[chunk][spot, 0] = recv[chunk][pairs_ref[to, 0]]
            stage[chunk][spot, 1] = recv[chunk][pairs_ref[to, 1]]
            pltpu.make_async_remote_copy(
                src_ref=stage[chunk].at[spot], dst_ref=owned_ref.at[chunk, place],
                send_sem=ssem2.at[chunk], recv_sem=rsem2.at[chunk],
                device_id={"chan": to}, device_id_type=MESH).start()
            return c

        lax.fori_loop(1, holders, route, 0)
        stage[chunk][place, 0] = recv[chunk][pairs_ref[me, 0]]
        stage[chunk][place, 1] = recv[chunk][pairs_ref[me, 1]]
        keep = pltpu.make_async_copy(
            stage[chunk].at[place], owned_ref.at[chunk, place], own.at[chunk])
        keep.start()
        kept.append(keep)

    for copy in pending:
        copy.wait_send()
    for copy in kept:
        copy.wait()
    for chunk in range(chunks):
        all_of(recv[chunk], ssem.at[chunk], n - 1).wait()
        all_of(stage[chunk], ssem2.at[chunk], holders - 1).wait()
        all_of(stage[chunk], rsem2.at[chunk], holders - 1).wait()


def exchange(x, pair_blocks, table, n):
    chans, windows, length = x.shape
    freqs = table.shape[0] // 2
    copies_held = 2 if n % 2 == 0 and n > 2 else 1
    holders = n // copies_held
    chunks = min(CHUNKS, freqs // holders)
    steps = radices(n)
    most = max(steps) - 1
    piece = (freqs // holders // chunks, 2 * windows, chans)
    bf, f32 = jnp.bfloat16, jnp.float32
    anywhere = pl.BlockSpec(memory_space=pl.ANY)
    dma = pltpu.SemaphoreType.DMA
    return pl.pallas_call(
        functools.partial(exchange_kernel, n, copies_held, chunks, steps),
        out_shape=jax.ShapeDtypeStruct((chunks, holders, 2) + piece, bf),
        in_specs=[anywhere, anywhere, anywhere],
        out_specs=anywhere,
        scratch_shapes=[
            pltpu.SMEM(pair_blocks.shape, jnp.int32),
            pltpu.VMEM(x.shape, bf),
            pltpu.VMEM(table.shape, bf),
            pltpu.VMEM((windows, chans, length), bf),
            pltpu.VMEM((windows, 2 * freqs, chans), f32),
            pltpu.VMEM((len(steps) + 1, windows, 2 * freqs), f32),
            pltpu.VMEM((len(steps), most, windows, 2 * freqs), f32),
            pltpu.VMEM((freqs * 2 * windows, chans), f32),
            pltpu.VMEM((holders, chunks) + piece, bf),
            dma((3,)), dma((chunks,)),
            dma((len(steps), most)), dma((len(steps), most)),
            dma((chunks,)), dma((chunks,)), dma((chunks,)), dma((chunks,)),
        ]
        + [pltpu.VMEM((n,) + piece, bf) for _ in range(chunks)]
        + [pltpu.VMEM((holders, 2) + piece, bf) for _ in range(chunks)],
        compiler_params=pltpu.CompilerParams(
            collective_id=0, has_side_effects=True, vmem_limit_bytes=60 * 1024 * 1024),
    )(pair_blocks, x, table)


def cross_kernel(scale, owned_ref, out_ref):
    chunks, group, _, bins, rows, chans = owned_ref.shape
    half = rows // 2
    exact = math.frexp(scale)[0] == 0.5
    for s in range(group):
        for c in range(chunks):
            for f in range(bins):
                first, second = owned_ref[c, s, 0, f], owned_ref[c, s, 1, f]
                if exact:
                    first = first * jnp.bfloat16(scale)
                turned = jnp.concatenate([-second[half:], second[:half]], axis=0)
                product = lax.dot_general(
                    first, jnp.concatenate([second, turned], axis=1),
                    (((0,), (0,)), ((), ())), preferred_element_type=jnp.float32)
                product = (product if exact else product * scale).astype(jnp.bfloat16)
                at = (s * chunks + c) * bins + f
                out_ref[0, at, 0] = product[:, :chans]
                out_ref[0, at, 1] = product[:, chans:]


def cross_spectra(owned, freqs, scale):
    chunks, n, two, bins, rows, chans = owned.shape
    group = max(1, 8 // (bins * chunks))
    return pl.pallas_call(
        functools.partial(cross_kernel, scale),
        grid=(n // group,),
        out_shape=jax.ShapeDtypeStruct((1, freqs, 2, chans, chans), jnp.bfloat16),
        in_specs=[pl.BlockSpec((chunks, group, two, bins, rows, chans), lambda i: (0, i, 0, 0, 0, 0))],
        out_specs=pl.BlockSpec((1, group * bins * chunks, 2, chans, chans), lambda i: (0, i, 0, 0, 0)),
        compiler_params=pltpu.CompilerParams(vmem_limit_bytes=60 * 1024 * 1024),
    )(owned)


def shards(samples, pair_blocks):
    windows, length = samples.shape[1:]
    n = lax.axis_size("chan")
    table = fourier_table(FREQS, length)
    owned = exchange(samples, pair_blocks, table, n)
    return cross_spectra(owned, FREQS, 1.0 / math.sqrt(windows))


def solution(mesh):
    placed = (P(("parts", "chan"), None, None), P("parts", None))
    return jax.shard_map(
        shards,
        mesh=mesh,
        in_specs=placed,
        out_specs=P(("parts", "chan"), None, None, None, None),
        check_vma=False,
    )
```

```python
import functools
import math

import jax
import jax.numpy as jnp
import ml_dtypes
import numpy as np
from jax import lax
from jax.experimental import pallas as pl
from jax.experimental.pallas import tpu as pltpu
from jax.sharding import PartitionSpec as P

FREQS = 128
BLOCK = 128
SMOOTH = 4
CHUNKS = 4
MESH = pl.DeviceIdType.MESH


def fourier_table(bins, length):
    positions = np.arange(length)
    turns = np.arange(1, bins + 1)[:, None] * positions[None, :] % length
    phase = 2.0 * np.pi * turns / length
    taper = 0.5 - 0.5 * np.cos(2.0 * np.pi * positions / length)
    table = np.concatenate([taper * np.cos(phase), -taper * np.sin(phase)], axis=0)
    return jnp.asarray(table.astype(np.float32).astype(ml_dtypes.bfloat16))


def radices(n):
    out = []
    while n > 1:
        r = 4 if n % 4 == 0 else (2 if n % 2 == 0 else n)
        out.append(r)
        n //= r
    return out


def split3(x):
    hi = x.astype(jnp.bfloat16)
    rest = x - hi.astype(jnp.float32)
    mid = rest.astype(jnp.bfloat16)
    lo = (rest - mid.astype(jnp.float32)).astype(jnp.bfloat16)
    return hi, mid, lo


NT = (((1,), (1,)), ((), ()))


def exchange_kernel(n, copies_held, chunks, steps, pairs_hbm, x_hbm, table_hbm, owned_ref, pairs_ref, x_ref,
                    table_ref, turned, spec, sums, gather, wide, send,
                    load, own, ssum, rsum, ssem, rsem, ssem2, rsem2, *bufs):
    recv, stage = bufs[:chunks], bufs[chunks:]
    holders = n // copies_held
    chans, windows, length = x_ref.shape
    freqs = table_ref.shape[0] // 2
    me = lax.axis_index("chan")
    place = lax.rem(me, holders)
    base = me - place

    fetch = pltpu.make_async_copy(x_hbm, x_ref, load.at[0])
    fetch.start()
    fetch_pairs = pltpu.make_async_copy(pairs_hbm, pairs_ref, load.at[1])
    fetch_pairs.start()
    fetch_table = pltpu.make_async_copy(table_hbm, table_ref, load.at[2])
    fetch_table.start()
    barrier = pltpu.get_barrier_semaphore()

    def greet(k, c):
        pl.semaphore_signal(barrier, inc=1, device_id={"chan": lax.rem(me + k, n)}, device_id_type=MESH)
        return c

    lax.fori_loop(1, n, greet, 0)

    which = lax.broadcasted_iota(jnp.int32, (windows, windows * chans), 1) % windows
    mine = lax.broadcasted_iota(jnp.int32, (windows, windows * chans), 0)
    pick = (which == mine).astype(jnp.float32).astype(jnp.bfloat16)
    fetch.wait()
    local = jnp.dot(
        pick, x_ref[...].reshape(windows * chans, length), preferred_element_type=jnp.float32
    )
    fetch_table.wait()
    sums[0] = sum(
        lax.dot_general(part, table_ref[...], NT, preferred_element_type=jnp.float32)
        for part in reversed(split3(local)))
    pl.semaphore_wait(barrier, n - 1)

    def sum_copy(phase, stride, radix, j):
        digit = lax.rem(me // stride, radix)
        other = me + (lax.rem(digit + j, radix) - digit) * stride
        return pltpu.make_async_remote_copy(
            src_ref=sums.at[phase], dst_ref=gather.at[phase, j - 1],
            send_sem=ssum.at[phase, j - 1], recv_sem=rsum.at[phase, j - 1],
            device_id={"chan": other}, device_id_type=MESH)

    pending = []
    stride = 1
    for phase, radix in enumerate(steps):
        copies = [sum_copy(phase, stride, radix, j) for j in range(1, radix)]
        for copy in copies:
            copy.start()
        if phase == 0:
            turned[...] = jnp.swapaxes(x_ref[...], 0, 1)
            for w in range(0, windows, 2):
                both = lax.dot_general(
                    table_ref[...], turned[w:w + 2].reshape(2 * chans, length), NT,
                    preferred_element_type=jnp.float32)
                spec[w] = both[:, :chans]
                spec[w + 1] = both[:, chans:]
        total = sums[phase]
        for j, copy in enumerate(copies):
            copy.wait_recv()
            total = total + gather[phase, j]
        sums[phase + 1] = total
        pending += copies
        stride *= radix
    common = (sums[len(steps)] / (chans * n)).T

    fi = lax.broadcasted_iota(jnp.int32, (freqs, freqs), 0)
    gi = lax.broadcasted_iota(jnp.int32, (freqs, freqs), 1)
    near = (jnp.abs(fi - gi) <= SMOOTH).astype(jnp.float32)
    weight = 1.0 / jnp.sum(near, axis=1, keepdims=True)
    near = near.astype(jnp.bfloat16)

    for w in range(windows):
        part = spec[w] - common[:, w:w + 1]
        re, im = part[:freqs], part[freqs:]
        amplitude = jnp.sqrt(re * re + im * im)
        hi = amplitude.astype(jnp.bfloat16)
        lo = (amplitude - hi.astype(jnp.float32)).astype(jnp.bfloat16)
        smoothed = (jnp.dot(near, hi, preferred_element_type=jnp.float32)
                    + jnp.dot(near, lo, preferred_element_type=jnp.float32)) * weight
        level = jnp.sum(amplitude, axis=0, keepdims=True) * (1.0 / freqs)
        scale = 1.0 / (smoothed + (0.05 * level + 1e-06))
        wide[pl.ds(w, freqs, stride=2 * windows), :] = re * scale
        wide[pl.ds(windows + w, freqs, stride=2 * windows), :] = im * scale
    send[...] = wide[...].astype(jnp.bfloat16).reshape(send.shape)

    for chunk in range(chunks):

        def give(k, c, chunk=chunk):
            to = lax.rem(me + n // 2 + k, n)

            @pl.when(to != me)
            def _():
                pltpu.make_async_remote_copy(
                    src_ref=send.at[lax.rem(to, holders), chunk], dst_ref=recv[chunk].at[me],
                    send_sem=ssem.at[chunk], recv_sem=rsem.at[chunk],
                    device_id={"chan": to}, device_id_type=MESH).start()

            return c

        lax.fori_loop(0, n, give, 0)
        recv[chunk][me] = send[place, chunk]

    kept = []

    def all_of(ref, sem, count):
        piece = ref.at[pl.ds(0, count)]
        return pltpu.make_async_copy(piece, piece, sem)

    fetch_pairs.wait()
    for chunk in range(chunks):
        all_of(recv[chunk], rsem.at[chunk], n - 1).wait()

        def route(k, c, chunk=chunk):
            spot = lax.rem(place + k, holders)
            to = base + spot
            stage[chunk][spot, 0] = recv[chunk][pairs_ref[to, 0]]
            stage[chunk][spot, 1] = recv[chunk][pairs_ref[to, 1]]
            pltpu.make_async_remote_copy(
                src_ref=stage[chunk].at[spot], dst_ref=owned_ref.at[chunk, place],
                send_sem=ssem2.at[chunk], recv_sem=rsem2.at[chunk],
                device_id={"chan": to}, device_id_type=MESH).start()
            return c

        lax.fori_loop(1, holders, route, 0)
        stage[chunk][place, 0] = recv[chunk][pairs_ref[me, 0]]
        stage[chunk][place, 1] = recv[chunk][pairs_ref[me, 1]]
        keep = pltpu.make_async_copy(
            stage[chunk].at[place], owned_ref.at[chunk, place], own.at[chunk])
        keep.start()
        kept.append(keep)

    for copy in pending:
        copy.wait_send()
    for copy in kept:
        copy.wait()
    for chunk in range(chunks):
        all_of(recv[chunk], ssem.at[chunk], n - 1).wait()
        all_of(stage[chunk], ssem2.at[chunk], holders - 1).wait()
        all_of(stage[chunk], rsem2.at[chunk], holders - 1).wait()


def exchange(x, pair_blocks, table, n):
    chans, windows, length = x.shape
    freqs = table.shape[0] // 2
    copies_held = 2 if n % 2 == 0 and n > 2 else 1
    holders = n // copies_held
    chunks = min(CHUNKS, freqs // holders)
    steps = radices(n)
    most = max(steps) - 1
    piece = (freqs // holders // chunks, 2 * windows, chans)
    bf, f32 = jnp.bfloat16, jnp.float32
    anywhere = pl.BlockSpec(memory_space=pl.ANY)
    dma = pltpu.SemaphoreType.DMA
    return pl.pallas_call(
        functools.partial(exchange_kernel, n, copies_held, chunks, steps),
        out_shape=jax.ShapeDtypeStruct((chunks, holders, 2) + piece, bf),
        in_specs=[anywhere, anywhere, anywhere],
        out_specs=pl.BlockSpec(memory_space=pltpu.VMEM),
        scratch_shapes=[
            pltpu.SMEM(pair_blocks.shape, jnp.int32),
            pltpu.VMEM(x.shape, bf),
            pltpu.VMEM(table.shape, bf),
            pltpu.VMEM((windows, chans, length), bf),
            pltpu.VMEM((windows, 2 * freqs, chans), f32),
            pltpu.VMEM((len(steps) + 1, windows, 2 * freqs), f32),
            pltpu.VMEM((len(steps), most, windows, 2 * freqs), f32),
            pltpu.VMEM((freqs * 2 * windows, chans), f32),
            pltpu.VMEM((holders, chunks) + piece, bf),
            dma((3,)), dma((chunks,)),
            dma((len(steps), most)), dma((len(steps), most)),
            dma((chunks,)), dma((chunks,)), dma((chunks,)), dma((chunks,)),
        ]
        + [pltpu.VMEM((n,) + piece, bf) for _ in range(chunks)]
        + [pltpu.VMEM((holders, 2) + piece, bf) for _ in range(chunks)],
        compiler_params=pltpu.CompilerParams(
            collective_id=0, has_side_effects=True, vmem_limit_bytes=60 * 1024 * 1024),
    )(pair_blocks, x, table)


def cross_kernel(scale, owned_ref, out_ref):
    chunks, group, _, bins, rows, chans = owned_ref.shape
    half = rows // 2
    exact = math.frexp(scale)[0] == 0.5
    for s in range(group):
        for c in range(chunks):
            for f in range(bins):
                first, second = owned_ref[c, s, 0, f], owned_ref[c, s, 1, f]
                if exact:
                    first = first * jnp.bfloat16(scale)
                turned = jnp.concatenate([-second[half:], second[:half]], axis=0)
                product = lax.dot_general(
                    first, jnp.concatenate([second, turned], axis=1),
                    (((0,), (0,)), ((), ())), preferred_element_type=jnp.float32)
                product = (product if exact else product * scale).astype(jnp.bfloat16)
                at = (s * chunks + c) * bins + f
                out_ref[0, at, 0] = product[:, :chans]
                out_ref[0, at, 1] = product[:, chans:]


def cross_spectra(owned, freqs, scale):
    chunks, n, two, bins, rows, chans = owned.shape
    group = max(1, 8 // (bins * chunks))
    return pl.pallas_call(
        functools.partial(cross_kernel, scale),
        grid=(n // group,),
        out_shape=jax.ShapeDtypeStruct((1, freqs, 2, chans, chans), jnp.bfloat16),
        in_specs=[pl.BlockSpec((chunks, group, two, bins, rows, chans), lambda i: (0, i, 0, 0, 0, 0))],
        out_specs=pl.BlockSpec((1, group * bins * chunks, 2, chans, chans), lambda i: (0, i, 0, 0, 0)),
        compiler_params=pltpu.CompilerParams(vmem_limit_bytes=32 * 1024 * 1024),
    )(owned)


def shards(samples, pair_blocks):
    windows, length = samples.shape[1:]
    n = lax.axis_size("chan")
    table = fourier_table(FREQS, length)
    owned = exchange(samples, pair_blocks, table, n)
    return cross_spectra(owned, FREQS, 1.0 / math.sqrt(windows))


def solution(mesh):
    placed = (P(("parts", "chan"), None, None), P("parts", None))
    return jax.shard_map(
        shards,
        mesh=mesh,
        in_specs=placed,
        out_specs=P(("parts", "chan"), None, None, None, None),
        check_vma=False,
    )
```
